512 devices in a mesh: train: 32 (over z, y_hi, core), feat: 4 (over y_lo), query: 4 (over x).
Axes of the slice: x: 4, y: 8 (y_hi: 2, y_lo: 4; y = y_hi * 4 + y_lo), z: 8, core: 2. Of those that a mesh axis runs over, the one named last changes fastest.
Arguments:
- queries: bfloat16 [1536, 8192], P('query', 'train'), may hold values from -6 to 6
- precond: bfloat16 [8192, 8192], P('train', 'feat'), may hold values from -0.125 to 0.125
- train_feats: bfloat16 [28672, 8192], P('train', 'feat'), may hold values from -6 to 6
- query_cluster: int32 [1536], P('query'), may hold values from 0 to 15
- train_shard: int32 [28672], P('train'), may hold values from 0 to 63
- pairs: int32 [256, 2], replicated, may hold values from 0 to 63, as said below
- log_weight: int32 [28672], P('train'), may hold values from -8 to 8
Outputs:
- query_influence: float32 [1536], P('query')
- train_influence: float32 [28672], P('train')
The draws below stay inside these ranges and needn't reach their ends.
Inputs may be any that keep to these rules, and one draw needn't show every extreme that they name: Rows are distinct pairs; the first entry is below 16, the second below 64.
All inputs are finite; a program needn't handle non-finite values.
Results may differ from the reference program's by a relative error of at most 0.0032.
Values may be sent and summed in bfloat16 or wider, within the bound.
No kernel may reach another device: no remote copies, remote signals or barrier semaphores. Data moves between devices by JAX's collectives and lax.ppermute only.
A program may use at most 64 MiB of HBM per device.

```python
import math
import jax
import jax.numpy as jnp
import numpy as np
from jax import lax

FEAT = 8192
TR_DEV = 896
CLUSTERS = 16
SHARDS = 64
NPAIRS = 256
NQ = 1536
NTRAIN = 28672


def draw_pairs(key, part):
    key = jax.random.fold_in(key, 7)
    chosen = jax.random.permutation(key, CLUSTERS * SHARDS)[:NPAIRS].astype(jnp.int32)
    return jnp.stack([chosen // SHARDS, chosen % SHARDS], axis=1).astype(jnp.int32)


def touch_ends(values, stream_key, smallest, top_value):
    shape = values.shape
    spot = [jax.random.randint(jax.random.fold_in(stream_key, axis), (), 0, shape[axis]) for axis in range(len(shape))]
    values = values.at[tuple(spot)].set(smallest)
    longest = shape.index(max(shape))
    spot[longest] = (spot[longest] + 1) % shape[longest]
    return values.at[tuple(spot)].set(top_value)


def with_spikes(array, stream_key, source, target, parts, factor):
    owner, partner = [(jnp.arange(array.shape[position]) // (array.shape[position] // parts)).reshape([-1 if axis == position else 1 for axis in range(array.ndim)]) for position in (source, target)]
    chosen = jax.random.permutation(stream_key, parts)[partner]
    strong = (owner == chosen) | (owner == (partner + parts // 2) % parts)
    return jnp.where(strong, factor * array, array)


def levels(stream_key, shape, split, low, top_value):
    def one(position, blocks):
        heights = jax.random.uniform(jax.random.fold_in(jax.random.fold_in(stream_key, 6), position), (blocks,), jnp.float32, low / len(split), top_value / len(split))
        return jnp.repeat(jnp.exp(heights), shape[position] // blocks).reshape((-1,) + (1,) * (len(shape) - position - 1))

    level = one(*split[0])
    for cut in split[1:]:
        level = level * one(*cut)
    return level


def rank_table(amount, lean):
    portions = [(1 << 20) // math.isqrt(grade ** lean) + 1 for grade in range(1, amount + 1)]
    spread = 1 + sum(portions) // (1 << 30)
    return np.cumsum(np.array([max(1, weight // spread) for weight in portions]))


def skewed_ids(rng, dims, amount, slope):
    listing = rank_table(amount, slope)
    pick = jax.random.randint(jax.random.fold_in(rng, 1), dims, 0, int(listing[amount - 1]))
    grade = jnp.searchsorted(jnp.asarray(listing, jnp.int32), pick, side="right")
    return jax.random.permutation(jax.random.fold_in(rng, 2), amount)[grade].astype(jnp.int32)


def gaussian(stream_key, shape, scale, most, cuts=(), held_as=jnp.bfloat16):
    entries = jax.random.normal(stream_key, shape, jnp.float32) * scale
    if len(cuts) > 0:
        entries = levels(stream_key, shape, cuts, -0.22, 0.18) * entries
    return jnp.clip(entries, min=-most, max=most).astype(held_as)


def bell_draw_with(own_key, shape, scale, reach, pieces, heavy, kind=jnp.bfloat16):
    result = scale * jax.random.normal(own_key, shape, jnp.float32)
    if pieces:
        result = result * levels(own_key, shape, pieces, -0.22, 0.18)
    return jnp.clip(with_spikes(result, jax.random.fold_in(own_key, 3), *heavy), -reach, reach).astype(kind)


def setup_inputs(seed: int = 0) -> dict:
    key_list = jax.random.split(jax.random.key(seed), 8)
    return {
        "queries": gaussian(key_list[0], (NQ, FEAT), 1.0, 6.0, ((0, 4), (1, 32))),
        "precond": bell_draw_with(key_list[1], (FEAT, FEAT), FEAT ** -0.5, 0.125, ((0, 32), (1, 4)), (0, 1, 32, 2.75)),
        "train_feats": gaussian(key_list[2], (NTRAIN, FEAT), 1.0, 6.0, ((0, 32), (1, 4))),
        "query_cluster": touch_ends(skewed_ids(key_list[3], (NQ,), CLUSTERS, 2), jax.random.fold_in(key_list[3], 3), 0, CLUSTERS - 1).astype(jnp.int32),
        "train_shard": touch_ends(skewed_ids(key_list[4], (NTRAIN,), SHARDS, 2), jax.random.fold_in(key_list[4], 3), 0, SHARDS - 1).astype(jnp.int32),
        "pairs": draw_pairs(jax.random.fold_in(key_list[7], 71), 0),
        "log_weight": touch_ends(jax.random.randint(key_list[6], (NTRAIN,), -8, 9), jax.random.fold_in(key_list[6], 1), -8, 8).astype(jnp.int32),
    }


def reference(queries, precond, train_feats, query_cluster, train_shard, pairs, log_weight):
    hi = lax.Precision.HIGHEST
    precond_q = jnp.dot(queries, precond, preferred_element_type=jnp.float32).astype(jnp.bfloat16)
    pair_c = (pairs[:, 0][:, None] == jnp.arange(CLUSTERS, dtype=jnp.int32)[None, :]).astype(jnp.float32)
    pair_s = (pairs[:, 1][:, None] == jnp.arange(SHARDS, dtype=jnp.int32)[None, :]).astype(jnp.float32)
    active = jnp.dot(pair_c.T, pair_s, precision=hi)
    query_hot = (query_cluster[:, None] == jnp.arange(CLUSTERS, dtype=jnp.int32)[None, :]).astype(jnp.float32)
    query_mask = jnp.dot(query_hot, active, precision=hi)
    weight = jnp.exp2(log_weight.astype(jnp.float32) * 0.25)
    scale = float(FEAT) ** -0.5
    blocks = NTRAIN // TR_DEV
    feat_blocks = train_feats.reshape(blocks, TR_DEV, FEAT)
    shard_blocks = train_shard.reshape(blocks, TR_DEV)
    weight_blocks = weight.reshape(blocks, TR_DEV)

    def one_block(items):
        feats, shards, weights = items
        score = lax.dot_general(precond_q, feats, (((1,), (1,)), ((), ())), preferred_element_type=jnp.float32) * scale
        shard_hot = (shards[:, None] == jnp.arange(SHARDS, dtype=jnp.int32)[None, :]).astype(jnp.float32) * weights[:, None]
        wmask = jnp.dot(query_mask, shard_hot.T, precision=hi)
        bounded = wmask * jnp.tanh(score)
        return jnp.sum(bounded, axis=1), jnp.sum(bounded, axis=0)

    query_parts, train_parts = lax.map(one_block, (feat_blocks, shard_blocks, weight_blocks))
    query_influence = jnp.sum(query_parts, axis=0) * float(NTRAIN) ** -0.5
    train_influence = train_parts.reshape(NTRAIN) * float(NQ) ** -0.5
    return query_influence, train_influence
```

```python
import jax
import jax.numpy as jnp
from jax import lax
from jax.sharding import Mesh, PartitionSpec as P

CLUSTERS = 16
SHARDS = 64
CORES = 2
Y_PARTS = 2
F32 = jnp.float32
BF16 = jnp.bfloat16
F16 = jnp.float16


def one_hot(ids, size):
    return (ids[:, None] == jnp.arange(size, dtype=jnp.int32)[None, :]).astype(BF16)


def other(x, axis, step=1):
    n = lax.axis_size(axis)
    return lax.ppermute(x, axis, [(i, i ^ step) for i in range(n)])


def to_all(x, axes, n):
    return lax.all_to_all(jnp.broadcast_to(x[None], (n,) + x.shape), axes, 0, 0)


def body(queries, precond, train_feats, query_cluster, train_shard, pairs, log_weight):
    n_z, n_f, n_q = lax.axis_size("z"), lax.axis_size("feat"), lax.axis_size("query")
    n_t = n_z * Y_PARTS
    core = lax.axis_index("c")
    lane = lax.axis_index("feat")
    query_rows, depth = queries.shape
    width = precond.shape[1]
    samples = train_feats.shape[0]
    feat = width * n_f
    half = query_rows // CORES
    rows = half // n_f

    mine = lax.dynamic_slice_in_dim(queries, core * half, half, 0)
    yours = lax.dynamic_slice_in_dim(queries, (1 - core) * half, half, 0)
    precond_other = other(precond, "c")
    theirs = other(yours, "c")
    part = jnp.dot(mine, precond, preferred_element_type=F32) + jnp.dot(
        theirs, precond_other, preferred_element_type=F32
    )
    up = 128.0
    pieces = (part * up).astype(F16).reshape(n_z, half // n_z, width)
    pieces, train_feats, train_shard, log_weight = lax.optimization_barrier(
        (pieces, train_feats, train_shard, log_weight)
    )
    feats_other = other(train_feats, "c")
    ids = jnp.stack([train_shard, log_weight])
    ids = jnp.concatenate([ids, other(ids, "c")], axis=1)
    pieces = lax.all_to_all(pieces, "z", 0, 0)
    block = jnp.sum(pieces.astype(F32), axis=0)
    sent = (block * (1.0 / n_z)).astype(F16)
    block = block * (1.0 / up) + other(sent, "yh").astype(F32) * (n_z / up)
    whole = lax.all_gather(block.astype(BF16), "z", axis=0, tiled=True)
    whole, feats_other = lax.optimization_barrier((whole, feats_other))

    dims = (((1,), (1,)), ((), ()))
    score = jnp.concatenate(
        [
            lax.dot_general(whole, train_feats, dims, preferred_element_type=F32).astype(BF16),
            lax.dot_general(whole, feats_other, dims, preferred_element_type=F32).astype(BF16),
        ],
        axis=1,
    )
    score = lax.all_to_all(score.reshape(n_f, rows, 2 * samples), "feat", 0, 0)
    score = jnp.sum(score.astype(F32), axis=0) * float(feat) ** (-0.5)

    active = jnp.minimum(
        lax.dot_general(
            one_hot(pairs[:, 0], CLUSTERS),
            one_hot(pairs[:, 1], SHARDS),
            (((0,), (0,)), ((), ())),
            preferred_element_type=F32,
        ),
        1.0,
    ).astype(BF16)
    clusters = lax.dynamic_slice_in_dim(query_cluster, core * half + lane * rows, rows, 0)
    query_mask = jnp.dot(one_hot(clusters, CLUSTERS), active, preferred_element_type=F32).astype(BF16)
    weight = jnp.exp2(ids[1].astype(F32) * 0.25)
    mask = lax.dot_general(query_mask, one_hot(ids[0], SHARDS), dims, preferred_element_type=F32)

    bounded = (mask * weight[None, :]) * jnp.tanh(score)
    by_query = jnp.sum(bounded, axis=1)
    by_sample = jnp.sum(bounded, axis=0)

    n_cf = CORES * n_f
    by_sample = by_sample.reshape(CORES, samples)
    by_sample = jnp.where(core == 0, by_sample, by_sample[::-1])
    both = jnp.concatenate([by_sample, jnp.broadcast_to(by_query[None], (CORES, rows))], axis=1)
    both = jnp.broadcast_to(both[None, :, None], (Y_PARTS, CORES, n_f, samples + rows))
    both = lax.all_to_all(both.reshape(Y_PARTS * n_cf, samples + rows), ("yh", "c", "feat"), 0, 0)
    both = both.reshape(Y_PARTS, n_cf, samples + rows)
    by_query = jnp.sum(both[:, :, samples:], axis=0).reshape(query_rows)
    by_sample = lax.dynamic_index_in_dim(both, lax.axis_index("yh"), 0, False)[:, :samples]
    by_sample = jnp.sum(by_sample, axis=0)

    both = to_all(jnp.concatenate([by_sample, by_query]), ("z", "query"), n_z * n_q)
    both = both.reshape(n_z, n_q, samples + query_rows)
    by_sample = lax.dynamic_index_in_dim(both, lax.axis_index("z"), 0, False)[:, :samples]
    by_query = lax.dynamic_index_in_dim(both, lax.axis_index("query"), 1, False)[:, samples:]
    by_sample = jnp.sum(by_sample, axis=0)
    by_query = jnp.sum(by_query, axis=0)
    all_queries = float(query_rows * n_q) ** (-0.5)
    all_samples = float(samples * n_t * CORES) ** (-0.5)
    return by_query * all_samples, by_sample * all_queries


def solution(mesh):
    n_train, n_feat, n_query = mesh.devices.shape
    fine = Mesh(
        mesh.devices.reshape(n_train // (Y_PARTS * CORES), Y_PARTS, CORES, n_feat, n_query),
        ("z", "yh", "c", "feat", "query"),
    )
    train = ("z", "yh", "c")
    return jax.shard_map(
        body,
        mesh=fine,
        in_specs=(
            P("query", train),
            P(train, "feat"),
            P(train, "feat"),
            P("query"),
            P(train),
            P(),
            P(train),
        ),
        out_specs=(P("query"), P(train)),
        check_vma=False,
    )
```

```python
import jax
import jax.numpy as jnp
from jax import lax
from jax.sharding import Mesh, PartitionSpec as P

CLUSTERS = 16
SHARDS = 64
CORES = 2
Y_PARTS = 2
F32 = jnp.float32
BF16 = jnp.bfloat16
F16 = jnp.float16


def one_hot(ids, size):
    return (ids[:, None] == jnp.arange(size, dtype=jnp.int32)[None, :]).astype(BF16)


def other(x, axis, step=1):
    n = lax.axis_size(axis)
    return lax.ppermute(x, axis, [(i, i ^ step) for i in range(n)])


def to_all(x, axes, n):
    return lax.all_to_all(jnp.broadcast_to(x[None], (n,) + x.shape), axes, 0, 0)


def body(queries, precond, train_feats, query_cluster, train_shard, pairs, log_weight):
    n_z, n_f, n_q = lax.axis_size("z"), lax.axis_size("feat"), lax.axis_size("query")
    n_t = n_z * Y_PARTS
    core = lax.axis_index("c")
    lane = lax.axis_index("feat")
    query_rows, depth = queries.shape
    width = precond.shape[1]
    samples = train_feats.shape[0]
    feat = width * n_f
    half = query_rows // CORES
    rows = half // n_f

    mine = lax.dynamic_slice_in_dim(queries, core * half, half, 0)
    yours = lax.dynamic_slice_in_dim(queries, (1 - core) * half, half, 0)
    precond_other = other(precond, "c")
    theirs = other(yours, "c")
    part = jnp.dot(mine, precond, preferred_element_type=F32) + jnp.dot(
        theirs, precond_other, preferred_element_type=F32
    )
    up = 128.0
    pieces = (part * up).astype(F16).reshape(n_z, half // n_z, width)
    pieces, train_feats, train_shard, log_weight = lax.optimization_barrier(
        (pieces, train_feats, train_shard, log_weight)
    )
    feats_other = other(train_feats, "c")
    ids = jnp.stack([train_shard, log_weight])
    ids = jnp.concatenate([ids, other(ids, "c")], axis=1)
    pieces = lax.all_to_all(pieces, "z", 0, 0)
    block = jnp.sum(pieces.astype(F32), axis=0)
    sent = (block * (1.0 / n_z)).astype(F16)
    block = block * (1.0 / up) + other(sent, "yh").astype(F32) * (n_z / up)
    whole = lax.all_gather(block.astype(BF16), "z", axis=0, tiled=True)
    whole, feats_other = lax.optimization_barrier((whole, feats_other))

    dims = (((1,), (1,)), ((), ()))
    score = jnp.concatenate(
        [
            lax.dot_general(whole, train_feats, dims, preferred_element_type=F32).astype(BF16),
            lax.dot_general(whole, feats_other, dims, preferred_element_type=F32).astype(BF16),
        ],
        axis=1,
    )
    score = lax.all_to_all(score.reshape(n_f, rows, 2 * samples), "feat", 0, 0)
    score = jnp.sum(score.astype(F32), axis=0) * float(feat) ** (-0.5)

    active = jnp.minimum(
        lax.dot_general(
            one_hot(pairs[:, 0], CLUSTERS),
            one_hot(pairs[:, 1], SHARDS),
            (((0,), (0,)), ((), ())),
            preferred_element_type=F32,
        ),
        1.0,
    ).astype(BF16)
    clusters = lax.dynamic_slice_in_dim(query_cluster, core * half + lane * rows, rows, 0)
    query_mask = jnp.dot(one_hot(clusters, CLUSTERS), active, preferred_element_type=F32).astype(BF16)
    weight = jnp.exp2(ids[1].astype(F32) * 0.25)
    mask = lax.dot_general(query_mask, one_hot(ids[0], SHARDS), dims, preferred_element_type=F32)

    bounded = (mask * weight[None, :]) * jnp.tanh(score)
    by_query = jnp.sum(bounded, axis=1)
    by_sample = jnp.sum(bounded, axis=0)

    by_sample = by_sample.reshape(CORES, samples)
    by_sample = jnp.where(core == 0, by_sample, by_sample[::-1])
    both = jnp.concatenate([by_sample, jnp.broadcast_to(by_query[None], (CORES, rows))], axis=1)
    both = jnp.broadcast_to(both[None, :, None], (Y_PARTS, CORES, n_f * n_q, samples + rows))
    both = both.reshape(Y_PARTS * CORES * n_f * n_q, samples + rows)
    both = lax.all_to_all(both, ("yh", "c", "feat", "query"), 0, 0)
    both = both.reshape(Y_PARTS, CORES * n_f, n_q, samples + rows)
    by_query = lax.dynamic_index_in_dim(both, lax.axis_index("query"), 2, False)[:, :, samples:]
    by_query = jnp.sum(by_query, axis=0).reshape(query_rows)
    by_sample = lax.dynamic_index_in_dim(both, lax.axis_index("yh"), 0, False)[:, :, :samples]
    by_sample = jnp.sum(by_sample, axis=(0, 1))

    by_query = jnp.sum(to_all(by_query, "z", n_z), axis=0)
    all_queries = float(query_rows * n_q) ** (-0.5)
    all_samples = float(samples * n_t * CORES) ** (-0.5)
    return by_query * all_samples, by_sample * all_queries


def solution(mesh):
    n_train, n_feat, n_query = mesh.devices.shape
    fine = Mesh(
        mesh.devices.reshape(n_train // (Y_PARTS * CORES), Y_PARTS, CORES, n_feat, n_query),
        ("z", "yh", "c", "feat", "query"),
    )
    train = ("z", "yh", "c")
    return jax.shard_map(
        body,
        mesh=fine,
        in_specs=(
            P("query", train),
            P(train, "feat"),
            P(train, "feat"),
            P("query"),
            P(train),
            P(),
            P(train),
        ),
        out_specs=(P("query"), P(train)),
        check_vma=False,
    )
```

```python
import jax
import jax.numpy as jnp
from jax import lax
from jax.sharding import Mesh, PartitionSpec as P

CLUSTERS = 16
SHARDS = 64
CORES = 2
Y_PARTS = 2
F32 = jnp.float32
BF16 = jnp.bfloat16
F16 = jnp.float16


def one_hot(ids, size):
    return (ids[:, None] == jnp.arange(size, dtype=jnp.int32)[None, :]).astype(BF16)


def other(x, axis, step=1):
    n = lax.axis_size(axis)
    return lax.ppermute(x, axis, [(i, i ^ step) for i in range(n)])


def to_all(x, axes, n):
    return lax.all_to_all(jnp.broadcast_to(x[None], (n,) + x.shape), axes, 0, 0)


def body(queries, precond, train_feats, query_cluster, train_shard, pairs, log_weight):
    n_z, n_f, n_q = lax.axis_size("z"), lax.axis_size("feat"), lax.axis_size("query")
    n_t = n_z * Y_PARTS
    core = lax.axis_index("c")
    lane = jnp.where(core == 0, lax.axis_index("feat"), n_f - 1 - lax.axis_index("feat"))
    query_rows, depth = queries.shape
    width = precond.shape[1]
    samples = train_feats.shape[0]
    feat = width * n_f
    half = query_rows // CORES
    rows = half // n_f

    mine = lax.dynamic_slice_in_dim(queries, core * half, half, 0)
    yours = lax.dynamic_slice_in_dim(queries, (1 - core) * half, half, 0)
    precond_other = other(precond, "c")
    theirs = other(yours, "c")
    part = jnp.dot(mine, precond, preferred_element_type=F32) + jnp.dot(
        theirs, precond_other, preferred_element_type=F32
    )
    up = 128.0
    pieces = (part * up).astype(F16).reshape(n_z, half // n_z, width)
    pieces, train_feats, train_shard, log_weight = lax.optimization_barrier(
        (pieces, train_feats, train_shard, log_weight)
    )
    feats_other = other(train_feats, "c")
    ids = jnp.stack([train_shard, log_weight])
    ids = jnp.concatenate([ids, other(ids, "c")], axis=1)
    lines = [[CORES * i for i in range(n_z)], [CORES * i + 1 for i in reversed(range(n_z))]]
    pieces = lax.all_to_all(pieces, ("z", "c"), 0, 0, axis_index_groups=lines)
    block = jnp.sum(pieces.astype(F32), axis=0)
    sent = (block * (1.0 / n_z)).astype(F16)
    block = block * (1.0 / up) + other(sent, "yh").astype(F32) * (n_z / up)
    whole = lax.all_gather(block.astype(BF16), ("z", "c"), axis=0, tiled=True, axis_index_groups=lines)
    whole, feats_other = lax.optimization_barrier((whole, feats_other))

    dims = (((1,), (1,)), ((), ()))
    score = jnp.concatenate(
        [
            lax.dot_general(whole, train_feats, dims, preferred_element_type=F32).astype(BF16),
            lax.dot_general(whole, feats_other, dims, preferred_element_type=F32).astype(BF16),
        ],
        axis=1,
    )
    lanes = [list(range(n_f)), [n_f + i for i in reversed(range(n_f))]]
    score = lax.all_to_all(score.reshape(n_f, rows, 2 * samples), ("c", "feat"), 0, 0, axis_index_groups=lanes)
    score = jnp.sum(score.astype(F32), axis=0) * float(feat) ** (-0.5)

    active = jnp.minimum(
        lax.dot_general(
            one_hot(pairs[:, 0], CLUSTERS),
            one_hot(pairs[:, 1], SHARDS),
            (((0,), (0,)), ((), ())),
            preferred_element_type=F32,
        ),
        1.0,
    ).astype(BF16)
    clusters = lax.dynamic_slice_in_dim(query_cluster, core * half + lane * rows, rows, 0)
    query_mask = jnp.dot(one_hot(clusters, CLUSTERS), active, preferred_element_type=F32).astype(BF16)
    weight = jnp.exp2(ids[1].astype(F32) * 0.25)
    mask = lax.dot_general(query_mask, one_hot(ids[0], SHARDS), dims, preferred_element_type=F32)

    bounded = (mask * weight[None, :]) * jnp.tanh(score)
    by_query = jnp.sum(bounded, axis=1)
    by_sample = jnp.sum(bounded, axis=0)

    n_cf = CORES * n_f
    by_sample = by_sample.reshape(CORES, samples)
    by_sample = jnp.where(core == 0, by_sample, by_sample[::-1])
    both = jnp.concatenate([by_sample, jnp.broadcast_to(by_query[None], (CORES, rows))], axis=1)
    both = jnp.broadcast_to(both[None, :, None], (Y_PARTS, CORES, n_f, samples + rows))
    both = lax.all_to_all(both.reshape(Y_PARTS * n_cf, samples + rows), ("yh", "c", "feat"), 0, 0)
    both = both.reshape(Y_PARTS, n_cf, samples + rows)
    by_query = jnp.sum(both[:, :, samples:], axis=0).reshape(CORES, n_f, rows)
    by_query = jnp.concatenate([by_query[0], by_query[1, ::-1]]).reshape(query_rows)
    by_sample = lax.dynamic_index_in_dim(both, lax.axis_index("yh"), 0, False)[:, :samples]
    by_sample = jnp.sum(by_sample, axis=0)

    both = to_all(jnp.concatenate([by_sample, by_query]), ("z", "query"), n_z * n_q)
    both = both.reshape(n_z, n_q, samples + query_rows)
    by_sample = lax.dynamic_index_in_dim(both, lax.axis_index("z"), 0, False)[:, :samples]
    by_query = lax.dynamic_index_in_dim(both, lax.axis_index("query"), 1, False)[:, samples:]
    by_sample = jnp.sum(by_sample, axis=0)
    by_query = jnp.sum(by_query, axis=0)
    all_queries = float(query_rows * n_q) ** (-0.5)
    all_samples = float(samples * n_t * CORES) ** (-0.5)
    return by_query * all_samples, by_sample * all_queries


def solution(mesh):
    n_train, n_feat, n_query = mesh.devices.shape
    fine = Mesh(
        mesh.devices.reshape(n_train // (Y_PARTS * CORES), Y_PARTS, CORES, n_feat, n_query),
        ("z", "yh", "c", "feat", "query"),
    )
    train = ("z", "yh", "c")
    return jax.shard_map(
        body,
        mesh=fine,
        in_specs=(
            P("query", train),
            P(train, "feat"),
            P(train, "feat"),
            P("query"),
            P(train),
            P(),
            P(train),
        ),
        out_specs=(P("query"), P(train)),
        check_vma=False,
    )
```

```python
import jax
import jax.numpy as jnp
from jax import lax
from jax.sharding import Mesh, PartitionSpec as P

CLUSTERS = 16
SHARDS = 64
CORES = 2
Y_PARTS = 2
F32 = jnp.float32
BF16 = jnp.bfloat16
F16 = jnp.float16


def one_hot(ids, size):
    return (ids[:, None] == jnp.arange(size, dtype=jnp.int32)[None, :]).astype(BF16)


def other(x, axis, step=1):
    n = lax.axis_size(axis)
    return lax.ppermute(x, axis, [(i, i ^ step) for i in range(n)])


def to_all(x, axes, n):
    return lax.all_to_all(jnp.broadcast_to(x[None], (n,) + x.shape), axes, 0, 0)


def body(queries, precond, train_feats, query_cluster, train_shard, pairs, log_weight):
    n_z, n_f, n_q = lax.axis_size("z"), lax.axis_size("feat"), lax.axis_size("query")
    n_t = n_z * Y_PARTS
    core = lax.axis_index("c")
    lane = jnp.where(core == 0, lax.axis_index("feat"), n_f - 1 - lax.axis_index("feat"))
    query_rows, depth = queries.shape
    width = precond.shape[1]
    samples = train_feats.shape[0]
    feat = width * n_f
    half = query_rows // CORES
    rows = half // n_f

    mine = lax.dynamic_slice_in_dim(queries, core * half, half, 0)
    yours = lax.dynamic_slice_in_dim(queries, (1 - core) * half, half, 0)
    precond_other = other(precond, "c")
    theirs = other(yours, "c")
    part = jnp.dot(mine, precond, preferred_element_type=F32) + jnp.dot(
        theirs, precond_other, preferred_element_type=F32
    )
    up = 128.0
    pieces = (part * up).astype(F16).reshape(n_z, half // n_z, width)
    pieces, train_feats, train_shard, log_weight = lax.optimization_barrier(
        (pieces, train_feats, train_shard, log_weight)
    )
    feats_other = other(train_feats, "c")
    ids = jnp.stack([train_shard, log_weight])
    ids = jnp.concatenate([ids, other(ids, "c")], axis=1)
    lines = [[CORES * i for i in range(n_z)], [CORES * i + 1 for i in reversed(range(n_z))]]
    pieces = lax.all_to_all(pieces, ("z", "c"), 0, 0, axis_index_groups=lines)
    block = jnp.sum(pieces.astype(F32), axis=0)
    sent = (block * (1.0 / n_z)).astype(F16)
    block = block * (1.0 / up) + other(sent, "yh").astype(F32) * (n_z / up)
    whole = lax.all_gather(block.astype(BF16), ("z", "c"), axis=0, tiled=True, axis_index_groups=lines)
    whole, feats_other = lax.optimization_barrier((whole, feats_other))

    dims = (((1,), (1,)), ((), ()))
    score = jnp.concatenate(
        [
            lax.dot_general(whole, train_feats, dims, preferred_element_type=F32).astype(BF16),
            lax.dot_general(whole, feats_other, dims, preferred_element_type=F32).astype(BF16),
        ],
        axis=1,
    )
    lanes = [list(range(n_f)), [n_f + i for i in reversed(range(n_f))]]
    score = lax.all_to_all(score.reshape(n_f, rows, 2 * samples), ("c", "feat"), 0, 0, axis_index_groups=lanes)
    score = jnp.sum(score.astype(F32), axis=0) * float(feat) ** (-0.5)

    active = jnp.minimum(
        lax.dot_general(
            one_hot(pairs[:, 0], CLUSTERS),
            one_hot(pairs[:, 1], SHARDS),
            (((0,), (0,)), ((), ())),
            preferred_element_type=F32,
        ),
        1.0,
    ).astype(BF16)
    clusters = lax.dynamic_slice_in_dim(query_cluster, core * half + lane * rows, rows, 0)
    query_mask = jnp.dot(one_hot(clusters, CLUSTERS), active, preferred_element_type=F32).astype(BF16)
    weight = jnp.exp2(ids[1].astype(F32) * 0.25)
    mask = lax.dot_general(query_mask, one_hot(ids[0], SHARDS), dims, preferred_element_type=F32)

    bounded = (mask * weight[None, :]) * jnp.tanh(score)
    by_query = jnp.sum(bounded, axis=1)
    by_sample = jnp.sum(bounded, axis=0)

    both = jnp.concatenate([by_sample[samples:], by_query])
    both = other(both, "c")
    by_sample = by_sample[:samples] + both[:samples]
    by_query, theirs = jnp.where(core == 0, by_query, both[samples:]), jnp.where(core == 0, both[samples:], by_query)

    both = to_all(jnp.concatenate([by_sample, by_query, theirs]), ("yh", "feat", "query"), Y_PARTS * n_f * n_q)
    both = both.reshape(Y_PARTS, n_f, n_q, samples + CORES * rows)
    by_query = lax.dynamic_index_in_dim(both, lax.axis_index("query"), 2, False)[:, :, samples:]
    by_query = jnp.sum(by_query, axis=0)
    by_query = jnp.concatenate([by_query[:, :rows], by_query[::-1, rows:]]).reshape(query_rows)
    by_sample = lax.dynamic_index_in_dim(both, lax.axis_index("yh"), 0, False)[:, :, :samples]
    by_sample = jnp.sum(by_sample, axis=(0, 1))

    by_query = jnp.sum(to_all(by_query, "z", n_z), axis=0)
    all_queries = float(query_rows * n_q) ** (-0.5)
    all_samples = float(samples * n_t * CORES) ** (-0.5)
    return by_query * all_samples, by_sample * all_queries


def solution(mesh):
    n_train, n_feat, n_query = mesh.devices.shape
    fine = Mesh(
        mesh.devices.reshape(n_train // (Y_PARTS * CORES), Y_PARTS, CORES, n_feat, n_query),
        ("z", "yh", "c", "feat", "query"),
    )
    train = ("z", "yh", "c")
    return jax.shard_map(
        body,
        mesh=fine,
        in_specs=(
            P("query", train),
            P(train, "feat"),
            P(train, "feat"),
            P("query"),
            P(train),
            P(),
            P(train),
        ),
        out_specs=(P("query"), P(train)),
        check_vma=False,
    )
```

```python
import jax
import jax.numpy as jnp
from jax import lax
from jax.sharding import Mesh, PartitionSpec as P

CLUSTERS = 16
SHARDS = 64
CORES = 2
Y_PARTS = 2
F32 = jnp.float32
BF16 = jnp.bfloat16
F16 = jnp.float16


def one_hot(ids, size):
    return (ids[:, None] == jnp.arange(size, dtype=jnp.int32)[None, :]).astype(BF16)


def other(x, axis, step=1):
    n = lax.axis_size(axis)
    return lax.ppermute(x, axis, [(i, i ^ step) for i in range(n)])


def to_all(x, axes, n):
    return lax.all_to_all(jnp.broadcast_to(x[None], (n,) + x.shape), axes, 0, 0)


def body(queries, precond, train_feats, query_cluster, train_shard, pairs, log_weight):
    n_z, n_f, n_q = lax.axis_size("z"), lax.axis_size("feat"), lax.axis_size("query")
    n_t = n_z * Y_PARTS
    core = lax.axis_index("c")
    lane = jnp.where(core == 0, lax.axis_index("feat"), n_f - 1 - lax.axis_index("feat"))
    query_rows, depth = queries.shape
    width = precond.shape[1]
    samples = train_feats.shape[0]
    feat = width * n_f
    half = query_rows // CORES
    rows = half // n_f

    mine = lax.dynamic_slice_in_dim(queries, core * half, half, 0)
    yours = lax.dynamic_slice_in_dim(queries, (1 - core) * half, half, 0)
    up = 128.0
    sent = (jnp.dot(yours, precond, preferred_element_type=F32) * (CORES * up)).astype(F16)
    sent, mine, train_feats, train_shard, log_weight = lax.optimization_barrier(
        (sent, mine, train_feats, train_shard, log_weight)
    )
    theirs = other(sent, "c")
    feats_other = other(train_feats, "c")
    ids = jnp.stack([train_shard, log_weight])
    ids = jnp.concatenate([ids, other(ids, "c")], axis=1)
    part = jnp.dot(mine, precond, preferred_element_type=F32) + theirs.astype(F32) * (1.0 / (CORES * up))
    pieces = (part * up).astype(F16).reshape(n_z, half // n_z, width)
    lines = [[CORES * i for i in range(n_z)], [CORES * i + 1 for i in reversed(range(n_z))]]
    pieces = lax.all_to_all(pieces, ("z", "c"), 0, 0, axis_index_groups=lines)
    block = jnp.sum(pieces.astype(F32), axis=0)
    sent = (block * (1.0 / n_z)).astype(F16)
    block = block * (1.0 / up) + other(sent, "yh").astype(F32) * (n_z / up)
    whole = lax.all_gather(block.astype(BF16), ("z", "c"), axis=0, tiled=True, axis_index_groups=lines)
    whole, feats_other = lax.optimization_barrier((whole, feats_other))

    dims = (((1,), (1,)), ((), ()))
    score = jnp.concatenate(
        [
            lax.dot_general(whole, train_feats, dims, preferred_element_type=F32).astype(BF16),
            lax.dot_general(whole, feats_other, dims, preferred_element_type=F32).astype(BF16),
        ],
        axis=1,
    )
    lanes = [list(range(n_f)), [n_f + i for i in reversed(range(n_f))]]
    score = lax.all_to_all(score.reshape(n_f, rows, 2 * samples), ("c", "feat"), 0, 0, axis_index_groups=lanes)
    score = jnp.sum(score.astype(F32), axis=0) * float(feat) ** (-0.5)

    active = jnp.minimum(
        lax.dot_general(
            one_hot(pairs[:, 0], CLUSTERS),
            one_hot(pairs[:, 1], SHARDS),
            (((0,), (0,)), ((), ())),
            preferred_element_type=F32,
        ),
        1.0,
    ).astype(BF16)
    clusters = lax.dynamic_slice_in_dim(query_cluster, core * half + lane * rows, rows, 0)
    query_mask = jnp.dot(one_hot(clusters, CLUSTERS), active, preferred_element_type=F32).astype(BF16)
    weight = jnp.exp2(ids[1].astype(F32) * 0.25)
    mask = lax.dot_general(query_mask, one_hot(ids[0], SHARDS), dims, preferred_element_type=F32)

    bounded = (mask * weight[None, :]) * jnp.tanh(score)
    by_query = jnp.sum(bounded, axis=1)
    by_sample = jnp.sum(bounded, axis=0)

    n_cf = CORES * n_f
    by_sample = by_sample.reshape(CORES, samples)
    by_sample = jnp.where(core == 0, by_sample, by_sample[::-1])
    both = jnp.concatenate([by_sample, jnp.broadcast_to(by_query[None], (CORES, rows))], axis=1)
    both = jnp.broadcast_to(both[None, :, None], (Y_PARTS, CORES, n_f, samples + rows))
    both = lax.all_to_all(both.reshape(Y_PARTS * n_cf, samples + rows), ("yh", "c", "feat"), 0, 0)
    both = both.reshape(Y_PARTS, n_cf, samples + rows)
    by_query = jnp.sum(both[:, :, samples:], axis=0).reshape(CORES, n_f, rows)
    by_query = jnp.concatenate([by_query[0], by_query[1, ::-1]]).reshape(query_rows)
    by_sample = lax.dynamic_index_in_dim(both, lax.axis_index("yh"), 0, False)[:, :samples]
    by_sample = jnp.sum(by_sample, axis=0)

    both = to_all(jnp.concatenate([by_sample, by_query]), ("z", "query"), n_z * n_q)
    both = both.reshape(n_z, n_q, samples + query_rows)
    by_sample = lax.dynamic_index_in_dim(both, lax.axis_index("z"), 0, False)[:, :samples]
    by_query = lax.dynamic_index_in_dim(both, lax.axis_index("query"), 1, False)[:, samples:]
    by_sample = jnp.sum(by_sample, axis=0)
    by_query = jnp.sum(by_query, axis=0)
    all_queries = float(query_rows * n_q) ** (-0.5)
    all_samples = float(samples * n_t * CORES) ** (-0.5)
    return by_query * all_samples, by_sample * all_queries


def solution(mesh):
    n_train, n_feat, n_query = mesh.devices.shape
    fine = Mesh(
        mesh.devices.reshape(n_train // (Y_PARTS * CORES), Y_PARTS, CORES, n_feat, n_query),
        ("z", "yh", "c", "feat", "query"),
    )
    train = ("z", "yh", "c")
    return jax.shard_map(
        body,
        mesh=fine,
        in_specs=(
            P("query", train),
            P(train, "feat"),
            P(train, "feat"),
            P("query"),
            P(train),
            P(),
            P(train),
        ),
        out_specs=(P("query"), P(train)),
        check_vma=False,
    )
```

```python
import jax
import jax.numpy as jnp
from jax import lax
from jax.sharding import Mesh, PartitionSpec as P

CLUSTERS = 16
SHARDS = 64
CORES = 2
Y_PARTS = 2
F32 = jnp.float32
BF16 = jnp.bfloat16
F16 = jnp.float16


def one_hot(ids, size):
    return (ids[:, None] == jnp.arange(size, dtype=jnp.int32)[None, :]).astype(BF16)


def other(x, axis, step=1):
    n = lax.axis_size(axis)
    return lax.ppermute(x, axis, [(i, i ^ step) for i in range(n)])


def to_all(x, axes, n):
    return lax.all_to_all(jnp.broadcast_to(x[None], (n,) + x.shape), axes, 0, 0)


def body(queries, precond, train_feats, query_cluster, train_shard, pairs, log_weight):
    n_z, n_f, n_q = lax.axis_size("z"), lax.axis_size("feat"), lax.axis_size("query")
    n_t = n_z * Y_PARTS
    core = lax.axis_index("c")
    lane = jnp.where(core == 0, lax.axis_index("feat"), n_f - 1 - lax.axis_index("feat"))
    query_rows, depth = queries.shape
    width = precond.shape[1]
    samples = train_feats.shape[0]
    feat = width * n_f
    half = query_rows // CORES
    rows = half // n_f

    mine = lax.dynamic_slice_in_dim(queries, core * half, half, 0)
    yours = lax.dynamic_slice_in_dim(queries, (1 - core) * half, half, 0)
    up = 128.0
    sent = (jnp.dot(yours, precond, preferred_element_type=F32) * (CORES * up)).astype(F16)
    sent, mine, train_feats, train_shard, log_weight = lax.optimization_barrier(
        (sent, mine, train_feats, train_shard, log_weight)
    )
    theirs = other(sent, "c")
    feats_other = other(train_feats, "c")
    ids = jnp.stack([train_shard, log_weight])
    ids = jnp.concatenate([ids, other(ids, "c")], axis=1)
    part = jnp.dot(mine, precond, preferred_element_type=F32) + theirs.astype(F32) * (1.0 / (CORES * up))
    pieces = (part * up).astype(F16).reshape(n_z, half // n_z, width)
    lines = [[(i + c * n_z // 2) % n_z * CORES + c for i in range(n_z)] for c in range(CORES)]
    pieces = lax.all_to_all(pieces, ("z", "c"), 0, 0, axis_index_groups=lines)
    block = jnp.sum(pieces.astype(F32), axis=0)
    sent = (block * (1.0 / n_z)).astype(F16)
    block = block * (1.0 / up) + other(sent, "yh").astype(F32) * (n_z / up)
    whole = lax.all_gather(block.astype(BF16), ("z", "c"), axis=0, tiled=True, axis_index_groups=lines)
    whole, feats_other = lax.optimization_barrier((whole, feats_other))

    dims = (((1,), (1,)), ((), ()))
    score = jnp.concatenate(
        [
            lax.dot_general(whole, train_feats, dims, preferred_element_type=F32).astype(BF16),
            lax.dot_general(whole, feats_other, dims, preferred_element_type=F32).astype(BF16),
        ],
        axis=1,
    )
    lanes = [list(range(n_f)), [n_f + i for i in reversed(range(n_f))]]
    score = lax.all_to_all(score.reshape(n_f, rows, 2 * samples), ("c", "feat"), 0, 0, axis_index_groups=lanes)
    score = jnp.sum(score.astype(F32), axis=0) * float(feat) ** (-0.5)

    active = jnp.minimum(
        lax.dot_general(
            one_hot(pairs[:, 0], CLUSTERS),
            one_hot(pairs[:, 1], SHARDS),
            (((0,), (0,)), ((), ())),
            preferred_element_type=F32,
        ),
        1.0,
    ).astype(BF16)
    clusters = lax.dynamic_slice_in_dim(query_cluster, core * half + lane * rows, rows, 0)
    query_mask = jnp.dot(one_hot(clusters, CLUSTERS), active, preferred_element_type=F32).astype(BF16)
    weight = jnp.exp2(ids[1].astype(F32) * 0.25)
    mask = lax.dot_general(query_mask, one_hot(ids[0], SHARDS), dims, preferred_element_type=F32)

    bounded = (mask * weight[None, :]) * jnp.tanh(score)
    by_query = jnp.sum(bounded, axis=1)
    by_sample = jnp.sum(bounded, axis=0)

    n_cf = CORES * n_f
    by_sample = by_sample.reshape(CORES, samples)
    by_sample = jnp.where(core == 0, by_sample, by_sample[::-1])
    both = jnp.concatenate([by_sample, jnp.broadcast_to(by_query[None], (CORES, rows))], axis=1)
    both = jnp.broadcast_to(both[None, :, None], (Y_PARTS, CORES, n_f, samples + rows))
    both = lax.all_to_all(both.reshape(Y_PARTS * n_cf, samples + rows), ("yh", "c", "feat"), 0, 0)
    both = both.reshape(Y_PARTS, n_cf, samples + rows)
    by_query = jnp.sum(both[:, :, samples:], axis=0).reshape(CORES, n_f, rows)
    by_query = jnp.concatenate([by_query[0], by_query[1, ::-1]]).reshape(query_rows)
    by_sample = lax.dynamic_index_in_dim(both, lax.axis_index("yh"), 0, False)[:, :samples]
    by_sample = jnp.sum(by_sample, axis=0)

    both = to_all(jnp.concatenate([by_sample, by_query]), ("z", "query"), n_z * n_q)
    both = both.reshape(n_z, n_q, samples + query_rows)
    by_sample = lax.dynamic_index_in_dim(both, lax.axis_index("z"), 0, False)[:, :samples]
    by_query = lax.dynamic_index_in_dim(both, lax.axis_index("query"), 1, False)[:, samples:]
    by_sample = jnp.sum(by_sample, axis=0)
    by_query = jnp.sum(by_query, axis=0)
    all_queries = float(query_rows * n_q) ** (-0.5)
    all_samples = float(samples * n_t * CORES) ** (-0.5)
    return by_query * all_samples, by_sample * all_queries


def solution(mesh):
    n_train, n_feat, n_query = mesh.devices.shape
    fine = Mesh(
        mesh.devices.reshape(n_train // (Y_PARTS * CORES), Y_PARTS, CORES, n_feat, n_query),
        ("z", "yh", "c", "feat", "query"),
    )
    train = ("z", "yh", "c")
    return jax.shard_map(
        body,
        mesh=fine,
        in_specs=(
            P("query", train),
            P(train, "feat"),
            P(train, "feat"),
            P("query"),
            P(train),
            P(),
            P(train),
        ),
        out_specs=(P("query"), P(train)),
        check_vma=False,
    )
```

```python
import jax
import jax.numpy as jnp
from jax import lax
from jax.sharding import Mesh, PartitionSpec as P

CLUSTERS = 16
SHARDS = 64
CORES = 2
Y_PARTS = 2
F32 = jnp.float32
BF16 = jnp.bfloat16
F16 = jnp.float16


def one_hot(ids, size):
    return (ids[:, None] == jnp.arange(size, dtype=jnp.int32)[None, :]).astype(BF16)


def other(x, axis, step=1):
    n = lax.axis_size(axis)
    return lax.ppermute(x, axis, [(i, i ^ step) for i in range(n)])


def to_all(x, axes, n):
    return lax.all_to_all(jnp.broadcast_to(x[None], (n,) + x.shape), axes, 0, 0)


def body(queries, precond, train_feats, query_cluster, train_shard, pairs, log_weight):
    n_z, n_f, n_q = lax.axis_size("z"), lax.axis_size("feat"), lax.axis_size("query")
    n_t = n_z * Y_PARTS
    core = lax.axis_index("c")
    turn = n_f // 2
    lane = lax.rem(lax.axis_index("feat") + core * (n_f - turn), n_f)
    query_rows, depth = queries.shape
    width = precond.shape[1]
    samples = train_feats.shape[0]
    feat = width * n_f
    half = query_rows // CORES
    rows = half // n_f

    mine = lax.dynamic_slice_in_dim(queries, core * half, half, 0)
    yours = lax.dynamic_slice_in_dim(queries, (1 - core) * half, half, 0)
    up = 128.0
    sent = (jnp.dot(yours, precond, preferred_element_type=F32) * (CORES * up)).astype(F16)
    sent, mine, train_feats, train_shard, log_weight = lax.optimization_barrier(
        (sent, mine, train_feats, train_shard, log_weight)
    )
    theirs = other(sent, "c")
    feats_other = other(train_feats, "c")
    ids = jnp.stack([train_shard, log_weight])
    ids = jnp.concatenate([ids, other(ids, "c")], axis=1)
    part = jnp.dot(mine, precond, preferred_element_type=F32) + theirs.astype(F32) * (1.0 / (CORES * up))
    pieces = (part * up).astype(F16).reshape(n_z, half // n_z, width)
    lines = [[(i + c * n_z // 2) % n_z * CORES + c for i in range(n_z)] for c in range(CORES)]
    pieces = lax.all_to_all(pieces, ("z", "c"), 0, 0, axis_index_groups=lines)
    block = jnp.sum(pieces.astype(F32), axis=0)
    sent = (block * (1.0 / n_z)).astype(F16)
    block = block * (1.0 / up) + other(sent, "yh").astype(F32) * (n_z / up)
    whole = lax.all_gather(block.astype(BF16), ("z", "c"), axis=0, tiled=True, axis_index_groups=lines)
    whole, feats_other = lax.optimization_barrier((whole, feats_other))

    dims = (((1,), (1,)), ((), ()))
    score = jnp.concatenate(
        [
            lax.dot_general(whole, train_feats, dims, preferred_element_type=F32).astype(BF16),
            lax.dot_general(whole, feats_other, dims, preferred_element_type=F32).astype(BF16),
        ],
        axis=1,
    )
    lanes = [[c * n_f + (i + c * turn) % n_f for i in range(n_f)] for c in range(CORES)]
    score = lax.all_to_all(score.reshape(n_f, rows, 2 * samples), ("c", "feat"), 0, 0, axis_index_groups=lanes)
    score = jnp.sum(score.astype(F32), axis=0) * float(feat) ** (-0.5)

    active = jnp.minimum(
        lax.dot_general(
            one_hot(pairs[:, 0], CLUSTERS),
            one_hot(pairs[:, 1], SHARDS),
            (((0,), (0,)), ((), ())),
            preferred_element_type=F32,
        ),
        1.0,
    ).astype(BF16)
    clusters = lax.dynamic_slice_in_dim(query_cluster, core * half + lane * rows, rows, 0)
    query_mask = jnp.dot(one_hot(clusters, CLUSTERS), active, preferred_element_type=F32).astype(BF16)
    weight = jnp.exp2(ids[1].astype(F32) * 0.25)
    mask = lax.dot_general(query_mask, one_hot(ids[0], SHARDS), dims, preferred_element_type=F32)

    bounded = (mask * weight[None, :]) * jnp.tanh(score)
    by_query = jnp.sum(bounded, axis=1)
    by_sample = jnp.sum(bounded, axis=0)

    n_cf = CORES * n_f
    by_sample = by_sample.reshape(CORES, samples)
    by_sample = jnp.where(core == 0, by_sample, by_sample[::-1])
    both = jnp.concatenate([by_sample, jnp.broadcast_to(by_query[None], (CORES, rows))], axis=1)
    both = jnp.broadcast_to(both[None, :, None], (Y_PARTS, CORES, n_f, samples + rows))
    both = lax.all_to_all(both.reshape(Y_PARTS * n_cf, samples + rows), ("yh", "c", "feat"), 0, 0)
    both = both.reshape(Y_PARTS, n_cf, samples + rows)
    by_query = jnp.sum(both[:, :, samples:], axis=0).reshape(CORES, n_f, rows)
    by_query = jnp.concatenate([by_query[0], by_query[1, turn:], by_query[1, :turn]]).reshape(query_rows)
    by_sample = lax.dynamic_index_in_dim(both, lax.axis_index("yh"), 0, False)[:, :samples]
    by_sample = jnp.sum(by_sample, axis=0)

    both = to_all(jnp.concatenate([by_sample, by_query]), ("z", "query"), n_z * n_q)
    both = both.reshape(n_z, n_q, samples + query_rows)
    by_sample = lax.dynamic_index_in_dim(both, lax.axis_index("z"), 0, False)[:, :samples]
    by_query = lax.dynamic_index_in_dim(both, lax.axis_index("query"), 1, False)[:, samples:]
    by_sample = jnp.sum(by_sample, axis=0)
    by_query = jnp.sum(by_query, axis=0)
    all_queries = float(query_rows * n_q) ** (-0.5)
    all_samples = float(samples * n_t * CORES) ** (-0.5)
    return by_query * all_samples, by_sample * all_queries


def solution(mesh):
    n_train, n_feat, n_query = mesh.devices.shape
    fine = Mesh(
        mesh.devices.reshape(n_train // (Y_PARTS * CORES), Y_PARTS, CORES, n_feat, n_query),
        ("z", "yh", "c", "feat", "query"),
    )
    train = ("z", "yh", "c")
    return jax.shard_map(
        body,
        mesh=fine,
        in_specs=(
            P("query", train),
            P(train, "feat"),
            P(train, "feat"),
            P("query"),
            P(train),
            P(),
            P(train),
        ),
        out_specs=(P("query"), P(train)),
        check_vma=False,
    )
```

```python
import jax
import jax.numpy as jnp
from jax import lax
from jax.sharding import Mesh, PartitionSpec as P

CLUSTERS = 16
SHARDS = 64
CORES = 2
Y_PARTS = 2
F32 = jnp.float32
BF16 = jnp.bfloat16
F16 = jnp.float16


def one_hot(ids, size):
    return (ids[:, None] == jnp.arange(size, dtype=jnp.int32)[None, :]).astype(BF16)


def other(x, axis, step=1):
    n = lax.axis_size(axis)
    return lax.ppermute(x, axis, [(i, i ^ step) for i in range(n)])


def to_all(x, axes, n):
    return lax.all_to_all(jnp.broadcast_to(x[None], (n,) + x.shape), axes, 0, 0)


def body(queries, precond, train_feats, query_cluster, train_shard, pairs, log_weight):
    n_z, n_f, n_q = lax.axis_size("z"), lax.axis_size("feat"), lax.axis_size("query")
    n_t = n_z * Y_PARTS
    core = lax.axis_index("c")
    turn = n_f // 2
    lane = lax.rem(lax.axis_index("feat") + core * (n_f - turn), n_f)
    query_rows, depth = queries.shape
    width = precond.shape[1]
    samples = train_feats.shape[0]
    feat = width * n_f
    half = query_rows // CORES
    rows = half // n_f

    mine = lax.dynamic_slice_in_dim(queries, core * half, half, 0)
    yours = lax.dynamic_slice_in_dim(queries, (1 - core) * half, half, 0)
    up = 128.0
    sent = (jnp.dot(yours, precond, preferred_element_type=F32) * (CORES * up)).astype(F16)
    sent, mine, train_feats, train_shard, log_weight = lax.optimization_barrier(
        (sent, mine, train_feats, train_shard, log_weight)
    )
    theirs = other(sent, "c")
    feats_other = other(train_feats, "c")
    ids = jnp.stack([train_shard, log_weight])
    ids = jnp.concatenate([ids, other(ids, "c")], axis=1)
    part = jnp.dot(mine, precond, preferred_element_type=F32) + theirs.astype(F32) * (1.0 / (CORES * up))
    pieces = (part * up).astype(F16).reshape(n_z, half // n_z, width)
    lines = [[i * CORES for i in range(n_z)], [(n_z // 2 - 1 - i) % n_z * CORES + 1 for i in range(n_z)]]
    pieces = lax.all_to_all(pieces, ("z", "c"), 0, 0, axis_index_groups=lines)
    block = jnp.sum(pieces.astype(F32), axis=0)
    sent = (block * (1.0 / n_z)).astype(F16)
    block = block * (1.0 / up) + other(sent, "yh").astype(F32) * (n_z / up)
    whole = lax.all_gather(block.astype(BF16), ("z", "c"), axis=0, tiled=True, axis_index_groups=lines)
    whole, feats_other = lax.optimization_barrier((whole, feats_other))

    dims = (((1,), (1,)), ((), ()))
    score = jnp.concatenate(
        [
            lax.dot_general(whole, train_feats, dims, preferred_element_type=F32).astype(BF16),
            lax.dot_general(whole, feats_other, dims, preferred_element_type=F32).astype(BF16),
        ],
        axis=1,
    )
    lanes = [[c * n_f + (i + c * turn) % n_f for i in range(n_f)] for c in range(CORES)]
    score = lax.all_to_all(score.reshape(n_f, rows, 2 * samples), ("c", "feat"), 0, 0, axis_index_groups=lanes)
    score = jnp.sum(score.astype(F32), axis=0) * float(feat) ** (-0.5)

    active = jnp.minimum(
        lax.dot_general(
            one_hot(pairs[:, 0], CLUSTERS),
            one_hot(pairs[:, 1], SHARDS),
            (((0,), (0,)), ((), ())),
            preferred_element_type=F32,
        ),
        1.0,
    ).astype(BF16)
    clusters = lax.dynamic_slice_in_dim(query_cluster, core * half + lane * rows, rows, 0)
    query_mask = jnp.dot(one_hot(clusters, CLUSTERS), active, preferred_element_type=F32).astype(BF16)
    weight = jnp.exp2(ids[1].astype(F32) * 0.25)
    mask = lax.dot_general(query_mask, one_hot(ids[0], SHARDS), dims, preferred_element_type=F32)

    bounded = (mask * weight[None, :]) * jnp.tanh(score)
    by_query = jnp.sum(bounded, axis=1)
    by_sample = jnp.sum(bounded, axis=0)

    n_cf = CORES * n_f
    by_sample = by_sample.reshape(CORES, samples)
    by_sample = jnp.where(core == 0, by_sample, by_sample[::-1])
    both = jnp.concatenate([by_sample, jnp.broadcast_to(by_query[None], (CORES, rows))], axis=1)
    both = jnp.broadcast_to(both[None, :, None], (Y_PARTS, CORES, n_f, samples + rows))
    both = lax.all_to_all(both.reshape(Y_PARTS * n_cf, samples + rows), ("yh", "c", "feat"), 0, 0)
    both = both.reshape(Y_PARTS, n_cf, samples + rows)
    by_query = jnp.sum(both[:, :, samples:], axis=0).reshape(CORES, n_f, rows)
    by_query = jnp.concatenate([by_query[0], by_query[1, turn:], by_query[1, :turn]]).reshape(query_rows)
    by_sample = lax.dynamic_index_in_dim(both, lax.axis_index("yh"), 0, False)[:, :samples]
    by_sample = jnp.sum(by_sample, axis=0)

    both = to_all(jnp.concatenate([by_sample, by_query]), ("z", "query"), n_z * n_q)
    both = both.reshape(n_z, n_q, samples + query_rows)
    by_sample = lax.dynamic_index_in_dim(both, lax.axis_index("z"), 0, False)[:, :samples]
    by_query = lax.dynamic_index_in_dim(both, lax.axis_index("query"), 1, False)[:, samples:]
    by_sample = jnp.sum(by_sample, axis=0)
    by_query = jnp.sum(by_query, axis=0)
    all_queries = float(query_rows * n_q) ** (-0.5)
    all_samples = float(samples * n_t * CORES) ** (-0.5)
    return by_query * all_samples, by_sample * all_queries


def solution(mesh):
    n_train, n_feat, n_query = mesh.devices.shape
    fine = Mesh(
        mesh.devices.reshape(n_train // (Y_PARTS * CORES), Y_PARTS, CORES, n_feat, n_query),
        ("z", "yh", "c", "feat", "query"),
    )
    train = ("z", "yh", "c")
    return jax.shard_map(
        body,
        mesh=fine,
        in_specs=(
            P("query", train),
            P(train, "feat"),
            P(train, "feat"),
            P("query"),
            P(train),
            P(),
            P(train),
        ),
        out_specs=(P("query"), P(train)),
        check_vma=False,
    )
```
